1024 devices in a mesh: dp: 16 (over y, z_hi, core), seq: 64 (over z_lo, x).
Axes of the slice: x: 4, y: 4, z: 32 (z_hi: 2, z_lo: 16; z = z_hi * 16 + z_lo), core: 2. Of those that a mesh axis runs over, the one named last changes fastest.
Arguments:
- qkv_teacher: bfloat16 [16, 3, 16, 512, 768], P('dp', None, None, 'seq'), may hold values from -5.2 to 5.2, as said below
- qkv_student: bfloat16 [16, 3, 16, 512, 768], P('dp', None, None, 'seq'), may hold values from -5.2 to 5.2, as said below
- proto_teacher: bfloat16 [768, 8192], P(None, 'seq'), may hold values from -0.21875 to 0.21875
- proto_student: bfloat16 [768, 8192], P(None, 'seq'), may hold values from -2.25 to 2.25
- center: float32 [8192], P('seq'), may hold values from -9 to 1
- pairing: int32 [16], replicated, may hold values from 0 to 15, as said below
Outputs:
- teacher_out: bfloat16 [16, 16, 512, 768], P('dp', None, 'seq')
- student_out: bfloat16 [16, 16, 512, 768], P('dp', None, 'seq')
- loss: float32 [16], P('dp')
The draws below stay inside these ranges and needn't reach their ends.
Inputs may be any that keep to these rules, and one draw needn't show every extreme that they name: `qkv_teacher`: random normal values; some positions of the keys may repeat a query's pattern. `qkv_student`: random normal values; some positions of the keys may repeat a query's pattern. pairing[pairing[v]] == v and pairing[v] != v for every view v.
All inputs are finite; a program needn't handle non-finite values.
Results may differ from the reference program's by a relative error of at most 0.001.
The reference program's roundings to bfloat16 on the way count: a program that leaves them out, or rounds other values in their place, can miss the bound.
Values may be sent and summed in bfloat16 or wider, within the bound.
A program may use at most 32 MiB of HBM per device.

```python
import jax
import jax.numpy as jnp
from jax import lax

HEADS = 12
HD = 64
F = 16
K = 8192
DA = 768
P_SIZE = 512
VIEWS = 16


def qkv_field(key):
    values = jnp.clip(jax.random.normal(key, (VIEWS, 3, F, P_SIZE, DA), jnp.float32), -5.0, 5.0)
    return values.astype(jnp.bfloat16)


def draw_qkv_teacher(key, part):
    return qkv_field(jax.random.fold_in(key, 11))


def draw_qkv_student(key, part):
    return qkv_field(jax.random.fold_in(key, 23))


def draw_proto_student(key, part):
    values = jnp.clip(jax.random.normal(key, (DA, K), jnp.float32), -5.0, 5.0) * DA ** (-0.5)
    values = jnp.clip(values, -2.2, 2.2)
    return values.astype(jnp.bfloat16)


def draw_center(key, part):
    values = jnp.clip(0.3 * jax.random.normal(key, (K,), jnp.float32), -1.0, 1.0)
    return values


def draw_pairing(key, part):
    order = jax.random.permutation(key, VIEWS).astype(jnp.int32)
    swapped = order.reshape(-1, 2)[:, ::-1].reshape(-1)
    return jnp.zeros((VIEWS,), jnp.int32).at[order].set(swapped)


def steps_of(stream_key, shape, shards, low, largest):
    loudness = 1.0
    for dim, parts in shards:
        heights = jax.random.uniform(jax.random.fold_in(jax.random.fold_in(stream_key, 6), dim), (parts,), jnp.float32, low / len(shards), largest / len(shards))
        loudness = loudness * jnp.repeat(jnp.exp(heights), shape[dim] // parts).reshape((-1,) + (1,) * (len(shape) - 1 - dim))
    return loudness


def scatter_about(own_key, extent, deviation, bound, cuts=(), held_as=jnp.bfloat16):
    level = steps_of(own_key, extent, cuts, -0.22, 0.18) if cuts else 1.0
    result = jax.random.normal(own_key, extent, jnp.float32) * deviation * level
    return jnp.minimum(jnp.maximum(result, -bound), bound).astype(held_as)


def setup_inputs(seed: int = 0) -> dict:
    splits = jax.random.split(jax.random.key(seed), 7)
    return {
        "qkv_teacher": draw_qkv_teacher(jax.random.fold_in(splits[6], 71), 0),
        "qkv_student": draw_qkv_student(jax.random.fold_in(splits[6], 71), 0),
        "proto_teacher": scatter_about(splits[2], (DA, K), DA ** -0.5, 0.21875, ((1, 64),)),
        "proto_student": draw_proto_student(jax.random.fold_in(splits[6], 71), 0),
        "center": draw_center(jax.random.fold_in(splits[6], 71), 0),
        "pairing": draw_pairing(jax.random.fold_in(splits[6], 71), 0),
    }


tau_teacher = 0.07
tau_student = 0.1
norm_eps = 1e-06

def attend_item(item):
    scores = lax.dot_general(item[0], item[1], (((1,), (1,)), ((), ())), preferred_element_type=jnp.float32) * HD ** (-0.5)
    weights = jax.nn.softmax(scores, axis=-1).astype(jnp.bfloat16)
    return jnp.dot(weights, item[2], preferred_element_type=jnp.float32).astype(jnp.bfloat16)

def view_attention(single_view):
    items = single_view.reshape(3, F, P_SIZE, HEADS, HD).transpose(1, 3, 0, 2, 4).reshape(F * HEADS, 3, P_SIZE, HD)
    outputs = lax.map(attend_item, items)
    return outputs.reshape(F, HEADS, P_SIZE, HD).transpose(0, 2, 1, 3).reshape(F, P_SIZE, HEADS * HD)

def unit_rows(values):
    return values * lax.rsqrt(lax.optimization_barrier(jnp.mean(values * values, axis=-1, keepdims=True)) + norm_eps)

def reference(qkv_teacher, qkv_student, proto_teacher, proto_student, center, pairing):
    teacher_out = lax.map(view_attention, qkv_teacher)
    student_out = lax.map(view_attention, qkv_student)
    scale = 1.0 / (F * P_SIZE)
    pooled_teacher = lax.optimization_barrier(jnp.sum(teacher_out.astype(jnp.float32), axis=(1, 2))) * scale
    pooled_student = lax.optimization_barrier(jnp.sum(student_out.astype(jnp.float32), axis=(1, 2))) * scale
    logit_teacher = jnp.dot(unit_rows(pooled_teacher), proto_teacher.astype(jnp.float32), precision=lax.Precision.HIGHEST)
    logit_student = jnp.dot(unit_rows(pooled_student), proto_student.astype(jnp.float32), precision=lax.Precision.HIGHEST)
    sharp = (logit_teacher - center[None, :]) / tau_teacher
    soft = logit_student / tau_student
    partner = sharp[pairing]
    probs = jax.nn.softmax(partner, axis=-1)
    loss = jax.nn.logsumexp(soft, axis=-1) - lax.optimization_barrier(jnp.sum(probs * soft, axis=-1))
    return (teacher_out, student_out, loss)
```

```python
import functools
import math

import jax
import jax.numpy as jnp
from jax import lax
from jax.experimental import pallas as pl
from jax.experimental.pallas import tpu as pltpu
from jax.sharding import PartitionSpec as P

HD = 64
NX = 4
PAIRS = 3
LANES = 128

tau_teacher = 0.07
tau_student = 0.1
norm_eps = 1e-06


def spread(step, n):
    return 1 + (n // 2 - 1 + step * (n // 4 if n >= 16 else 1)) % (n - 1)


def drain(ref, sem):
    pltpu.make_async_copy(ref, ref, sem).wait()


def unit_vector(values):
    return values * lax.rsqrt(jnp.mean(values * values) + norm_eps)


def exact_dot(row, matrix):
    high = row.astype(jnp.bfloat16).astype(jnp.float32)
    rest = row - high
    middle = rest.astype(jnp.bfloat16).astype(jnp.float32)
    low = rest - middle
    index = lax.broadcasted_iota(jnp.int32, (8, row.shape[1]), 0)
    parts = jnp.where(index == 0, high, jnp.where(index == 1, middle, jnp.where(index == 2, low, 0.0)))
    products = jnp.dot(parts.astype(jnp.bfloat16), matrix, preferred_element_type=jnp.float32)
    return jnp.sum(products, axis=0, keepdims=True)


def merge(stats):
    lane = lax.broadcasted_iota(jnp.int32, stats.shape, 2)

    def column(i):
        return jnp.sum(jnp.where(lane == i, stats, 0.0), axis=2, keepdims=True)

    top_teacher, top_student = column(0), column(3)
    best_teacher = jnp.max(top_teacher, axis=0, keepdims=True)
    best_student = jnp.max(top_student, axis=0, keepdims=True)
    weight = jnp.exp(top_teacher - best_teacher)
    share = jnp.exp(top_student - best_student)
    return (
        best_teacher[0],
        jnp.sum(column(1) * weight, axis=0),
        jnp.sum(column(2) * weight, axis=0),
        best_student[0],
        jnp.sum(column(4) * share, axis=0),
    )


def packed(values):
    lane = lax.broadcasted_iota(jnp.int32, (1, LANES), 1)
    row = jnp.zeros((1, LANES), jnp.float32)
    for i, value in enumerate(values):
        row = jnp.where(lane == i, value, row)
    return row


def kernel(
    nz, ndp,
    qkv_t, qkv_s, proto_t, proto_s, center, pairing,
    out, loss,
    inp, xb, zb, ob, rb, pool, zpool, mine, xpool, row_t, all_t, stat, zstat, xstat,
    in_sem, x_send, x_recv, z_send, z_recv, rz_send, rz_recv, rx_send, rx_recv, s_send, s_recv,
):
    view = lax.axis_index("dp")
    me = lax.axis_index("seq")
    x = me % NX
    z = me // NX
    width = PAIRS * LANES

    def at_x(d):
        return {"seq": z * NX + (x + d) % NX}

    def at_z(d):
        return {"seq": (z + d) % nz * NX + x}

    def lanes_of(owner, u):
        return pl.ds(pl.multiple_of(owner % 2 * width + u * LANES, LANES), LANES)

    def remote(src, dst, send, recv, where):
        pltpu.make_async_remote_copy(
            src_ref=src, dst_ref=dst, send_sem=send, recv_sem=recv,
            device_id=where, device_id_type=pl.DeviceIdType.MESH,
        ).start()

    def each(n, body):
        lax.fori_loop(0, n, lambda i, c: (body(i), c)[1], 0)

    loads = [
        pltpu.make_async_copy(qkv_t, inp.at[pl.ds(0, 1)], in_sem.at[0]),
        pltpu.make_async_copy(qkv_s, inp.at[pl.ds(1, 1)], in_sem.at[1]),
    ]
    for load in loads:
        load.start()
    barrier = pltpu.get_barrier_semaphore()

    def greet(where):
        pl.semaphore_signal(barrier, inc=1, device_id=where, device_id_type=pl.DeviceIdType.MESH)

    each(nz - 1, lambda i: greet(at_z(i + 1)))
    each(NX - 1, lambda i: greet(at_x(i + 1)))
    each(ndp - 1, lambda i: greet({"dp": (view + i + 1) % ndp}))
    pl.semaphore_wait(barrier, nz - 1 + NX - 1 + ndp - 1)
    for load in loads:
        load.wait()

    def send_x(u):
        for d in range(1, NX):
            owner = (x + d) % NX
            remote(
                inp.at[owner // 2, :, :, :, lanes_of(owner, u)],
                xb.at[u, :, :, NX - 1 - d],
                x_send.at[u], x_recv.at[u], at_x(d),
            )

    def send_own(u):
        def body(i):
            d = spread(i, nz)
            remote(
                inp.at[x // 2, :, (z + d) % nz, :, lanes_of(x, u)],
                zb.at[u, :, z, 0],
                z_send.at[u], z_recv.at[u], at_z(d),
            )

        each(nz - 1, body)
        pltpu.make_async_copy(
            inp.at[x // 2, :, z, :, lanes_of(x, u)], zb.at[u, :, z, 0], z_recv.at[u]
        ).start()

    def send_on(u):
        drain(xb.at[u], x_recv.at[u])

        def body(i):
            d = spread(i, nz)
            remote(
                xb.at[u, :, (z + d) % nz],
                zb.at[u, :, z, pl.ds(1, NX - 1)],
                z_send.at[u], z_recv.at[u], at_z(d),
            )

        each(nz - 1, body)
        pltpu.make_async_copy(
            xb.at[u, :, z], zb.at[u, :, z, pl.ds(1, NX - 1)], z_recv.at[u]
        ).start()

    each(PAIRS, send_x)
    each(PAIRS, send_own)
    each(PAIRS, send_on)

    rows = nz * NX * 8
    block = min(rows, 128)
    rate = HD ** (-0.5) * math.log2(math.e)

    def attend(u):
        drain(zb.at[u], z_recv.at[u])
        flat = lambda ref: ref[...].astype(jnp.float32).reshape(-1, LANES)
        keys = flat(zb.at[u, 1]).astype(jnp.bfloat16)
        values = flat(zb.at[u, 2]).astype(jnp.bfloat16)
        per = block // (NX * 8)
        lane = lax.broadcasted_iota(jnp.int32, (block, LANES), 1)

        def body(i, total):
            query = flat(zb.at[u, 0, pl.ds(i * per, per)])
            halves = []
            for head in range(2):
                own = (lane >= HD) == (head == 1)
                scores = lax.dot_general(
                    jnp.where(own, query, 0.0).astype(jnp.bfloat16), keys,
                    (((1,), (1,)), ((), ())), preferred_element_type=jnp.float32,
                )
                raised = jnp.exp2((scores - jnp.max(scores, axis=1, keepdims=True)) * rate)
                share = 1.0 / jnp.sum(raised, axis=1, keepdims=True)
                halves.append(
                    jnp.dot((raised * share).astype(jnp.bfloat16), values, preferred_element_type=jnp.float32)
                )
            result = jnp.where(lane >= HD, halves[1], halves[0])
            rounded = result.reshape(per, NX, 8, LANES).astype(jnp.bfloat16)
            ob[u, pl.ds(i * per, per)] = rounded
            return total + jnp.sum(
                rounded.astype(jnp.float32).reshape(block, LANES), axis=0, keepdims=True
            )

        pool[u] = lax.fori_loop(0, rows // block, body, jnp.zeros((1, LANES), jnp.float32))

    def send_back(u):
        def body(i):
            d = spread(i, nz)
            remote(ob.at[u, (z + d) % nz], rb.at[u, z], rz_send.at[u], rz_recv.at[u], at_z(d))

        each(nz - 1, body)
        pltpu.make_async_copy(ob.at[u, z], rb.at[u, z], rz_recv.at[u]).start()

    def gather(src, dst, slot, n, where, k):
        def body(i):
            remote(src, dst.at[slot], s_send.at[k], s_recv.at[k], where(i + 1))

        each(n - 1, body)
        pltpu.make_async_copy(src, dst.at[slot], s_recv.at[k]).start()
        drain(dst, s_recv.at[k])

    each(PAIRS - 1, lambda u: (attend(u), send_back(u)))
    attend(PAIRS - 1)
    send_back(PAIRS - 1)

    gather(pool, zpool, z, nz, at_z, 0)
    pool_sum = jnp.sum(zpool[...], axis=0) * (1.0 / (nz * rows))
    mine[...] = pool_sum
    gather(mine, xpool, x, NX, at_x, 1)
    pooled = [
        jnp.concatenate([xpool[2 * s + h, u] for h in range(2) for u in range(PAIRS)], axis=1)
        for s in range(2)
    ]
    sharp = (exact_dot(unit_vector(pooled[0]), proto_t[...]) - center[...]) * (1.0 / tau_teacher)
    soft = exact_dot(unit_vector(pooled[1]), proto_s[...]) * (1.0 / tau_student)
    row_t[...] = sharp
    gather(row_t, all_t, view, ndp, lambda d: {"dp": (view + d) % ndp}, 2)

    def send_home(u):
        drain(rb.at[u], rz_recv.at[u])
        for d in range(1, NX):
            remote(
                rb.at[u, :, d], out.at[x // 2, 0, :, :, lanes_of(x, u)],
                rx_send.at[u], rx_recv, at_x(d),
            )
        pltpu.make_async_copy(
            rb.at[u, :, 0], out.at[x // 2, 0, :, :, lanes_of(x, u)], rx_recv
        ).start()

    each(PAIRS - 1, send_home)

    partner = all_t[pairing[view]]
    top_teacher = jnp.max(partner, axis=1, keepdims=True)
    raised = jnp.exp(partner - top_teacher)
    top_student = jnp.max(soft, axis=1, keepdims=True)
    stat[0] = packed(
        (
            top_teacher,
            jnp.sum(raised, axis=1, keepdims=True),
            jnp.sum(raised * soft, axis=1, keepdims=True),
            top_student,
            jnp.sum(jnp.exp(soft - top_student), axis=1, keepdims=True),
        )
    )
    gather(stat.at[0], zstat, z, nz, at_z, 3)
    stat[1] = packed(merge(zstat[...]))
    send_home(PAIRS - 1)
    gather(stat.at[1], xstat, x, NX, at_x, 4)
    _, total_teacher, product, best_student, total_student = merge(xstat[...])
    value = best_student + jnp.log(total_student) - product / total_teacher
    loss[0] = jnp.sum(value)

    drain(out, rx_recv)

    def finish(u):
        drain(xb.at[u], x_send.at[u])
        drain(zb.at[u, :, pl.ds(0, nz - 1)], z_send.at[u])
        drain(rb.at[u, pl.ds(0, nz - 1)], rz_send.at[u])
        drain(rb.at[u, :, pl.ds(0, NX - 1)], rx_send.at[u])

    each(PAIRS, finish)
    drain(zpool.at[pl.ds(0, nz - 1)], s_send.at[0])
    drain(xpool.at[pl.ds(0, NX - 1)], s_send.at[1])
    drain(all_t.at[pl.ds(0, ndp - 1)], s_send.at[2])
    drain(zstat.at[pl.ds(0, nz - 1)], s_send.at[3])
    drain(xstat.at[pl.ds(0, NX - 1)], s_send.at[4])


def local(nz, ndp, qkv_teacher, qkv_student, proto_teacher, proto_student, center, pairing):
    frames, rows, features = qkv_teacher.shape[2:]
    bf16, f32 = jnp.bfloat16, jnp.float32
    dma = pltpu.SemaphoreType.DMA
    anywhere = pl.BlockSpec(memory_space=pl.ANY)
    vmem = pl.BlockSpec(memory_space=pltpu.VMEM)
    smem = pl.BlockSpec(memory_space=pltpu.SMEM)
    out, loss = pl.pallas_call(
        functools.partial(kernel, nz, ndp),
        out_shape=(
            jax.ShapeDtypeStruct((2, 1, frames, rows, features), bf16),
            jax.ShapeDtypeStruct((1,), f32),
        ),
        in_specs=[anywhere, anywhere, vmem, vmem, vmem, smem],
        out_specs=(anywhere, smem),
        scratch_shapes=[
            pltpu.VMEM((2, 3, frames, rows, features), bf16),
            pltpu.VMEM((PAIRS, 3, nz, NX - 1, rows, LANES), bf16),
            pltpu.VMEM((PAIRS, 3, nz, NX, rows, LANES), bf16),
            pltpu.VMEM((PAIRS, nz, NX, rows, LANES), bf16),
            pltpu.VMEM((PAIRS, nz, NX, rows, LANES), bf16),
            pltpu.VMEM((PAIRS, 1, LANES), f32),
            pltpu.VMEM((nz, PAIRS, 1, LANES), f32),
            pltpu.VMEM((PAIRS, 1, LANES), f32),
            pltpu.VMEM((NX, PAIRS, 1, LANES), f32),
            pltpu.VMEM((1, LANES), f32),
            pltpu.VMEM((ndp, 1, LANES), f32),
            pltpu.VMEM((2, 1, LANES), f32),
            pltpu.VMEM((nz, 1, LANES), f32),
            pltpu.VMEM((NX, 1, LANES), f32),
            dma((2,)),
            dma((PAIRS,)), dma((PAIRS,)),
            dma((PAIRS,)), dma((PAIRS,)),
            dma((PAIRS,)), dma((PAIRS,)),
            dma((PAIRS,)), dma(()),
            dma((5,)), dma((5,)),
        ],
        compiler_params=pltpu.CompilerParams(
            collective_id=0, has_side_effects=True, vmem_limit_bytes=40 * 1024 * 1024
        ),
        name="views",
    )(qkv_teacher, qkv_student, proto_teacher, proto_student, center.reshape(1, -1), pairing)
    return out[0], out[1], loss


def solution(mesh):
    wide = P("dp", None, None, "seq", None)
    return jax.shard_map(
        functools.partial(local, mesh.shape["seq"] // NX, mesh.shape["dp"]),
        mesh=mesh,
        in_specs=(wide, wide, P(None, "seq"), P(None, "seq"), P("seq"), P()),
        out_specs=(P("dp", None, "seq", None), P("dp", None, "seq", None), P("dp")),
        check_vma=False,
    )
```

```python
import functools
import math

import jax
import jax.numpy as jnp
from jax import lax
from jax.experimental import pallas as pl
from jax.experimental.pallas import tpu as pltpu
from jax.sharding import PartitionSpec as P

HD = 64
NX = 4
NH, NC = 2, 2
PAIRS = 3
LANES = 128

tau_teacher = 0.07
tau_student = 0.1
norm_eps = 1e-06


def spread(step, n):
    return 1 + (n // 2 - 1 + step * (n // 4 if n >= 16 else 1)) % (n - 1)


def drain(ref, sem):
    pltpu.make_async_copy(ref, ref, sem).wait()


def unit_vector(values):
    return values * lax.rsqrt(jnp.mean(values * values) + norm_eps)


def exact_dot(row, matrix):
    high = row.astype(jnp.bfloat16).astype(jnp.float32)
    rest = row - high
    middle = rest.astype(jnp.bfloat16).astype(jnp.float32)
    low = rest - middle
    index = lax.broadcasted_iota(jnp.int32, (8, row.shape[1]), 0)
    parts = jnp.where(index == 0, high, jnp.where(index == 1, middle, jnp.where(index == 2, low, 0.0)))
    products = jnp.dot(parts.astype(jnp.bfloat16), matrix, preferred_element_type=jnp.float32)
    return jnp.sum(products, axis=0, keepdims=True)


def merge(stats):
    lane = lax.broadcasted_iota(jnp.int32, stats.shape, 2)

    def column(i):
        return jnp.sum(jnp.where(lane == i, stats, 0.0), axis=2, keepdims=True)

    top_teacher, top_student = column(0), column(3)
    best_teacher = jnp.max(top_teacher, axis=0, keepdims=True)
    best_student = jnp.max(top_student, axis=0, keepdims=True)
    weight = jnp.exp(top_teacher - best_teacher)
    share = jnp.exp(top_student - best_student)
    return (
        best_teacher[0],
        jnp.sum(column(1) * weight, axis=0),
        jnp.sum(column(2) * weight, axis=0),
        best_student[0],
        jnp.sum(column(4) * share, axis=0),
    )


def packed(values):
    lane = lax.broadcasted_iota(jnp.int32, (1, LANES), 1)
    row = jnp.zeros((1, LANES), jnp.float32)
    for i, value in enumerate(values):
        row = jnp.where(lane == i, value, row)
    return row


def kernel(
    nz, ndp,
    qkv_t, qkv_s, proto_t, proto_s, center, pairing,
    out, loss,
    inp, protos, middle, pairs, xb, zb, ob, hb, pool, zpool, mine, xpool, stat, zstat, xstat,
    in_sem, x_send, x_recv, z_send, z_recv, h_send, h_recv, o_send, o_recv, s_send, s_recv,
):
    view = lax.axis_index("dp")
    me = lax.axis_index("seq")
    x = me % NX
    z = me // NX
    y, half, core = view // (NH * NC), view // NC % NH, view % NC
    ring, turn = NH * nz, half * nz + z
    plane, spot = ndp // NH * NX, (y * NC + core) * NX + x
    width = PAIRS * LANES

    def at_x(d):
        return {"seq": z * NX + (x + d) % NX}

    def at_z(d):
        return {"seq": (z + d) % nz * NX + x}

    def at_ring(d):
        to = (turn + d) % ring
        return {"dp": (y * NH + to // nz) * NC + core, "seq": to % nz * NX + x}

    def at_plane(d):
        to = (spot + d) % plane
        row = to // NX
        return {"dp": (row // NC * NH + half) * NC + row % NC, "seq": z * NX + to % NX}

    def lanes_of(owner, u):
        return pl.ds(pl.multiple_of(owner % 2 * width + u * LANES, LANES), LANES)

    def remote(src, dst, send, recv, where):
        pltpu.make_async_remote_copy(
            src_ref=src, dst_ref=dst, send_sem=send, recv_sem=recv,
            device_id=where, device_id_type=pl.DeviceIdType.MESH,
        ).start()

    def span(first, last, body):
        lax.fori_loop(first, last, lambda i, c: (body(i), c)[1], 0)

    def each(n, body):
        span(0, n, body)

    def far_first(i, n):
        return 1 + (n // 2 - 1 + i) % (n - 1)

    barrier = pltpu.get_barrier_semaphore()

    def greet(where):
        pl.semaphore_signal(barrier, inc=1, device_id=where, device_id_type=pl.DeviceIdType.MESH)

    each(ring - 1, lambda i: greet(at_ring(far_first(i, ring))))
    each(plane - 1, lambda i: greet(at_plane(i + 1)))
    loads = [
        pltpu.make_async_copy(src, dst, in_sem.at[i])
        for i, (src, dst) in enumerate(
            (
                (qkv_t, inp.at[pl.ds(0, 1)]),
                (qkv_s, inp.at[pl.ds(1, 1)]),
                (proto_t, protos.at[0]),
                (proto_s, protos.at[1]),
                (center, middle),
                (pairing, pairs),
            )
        )
    ]
    for load in loads:
        load.start()
    for load in loads:
        load.wait()
    pl.semaphore_wait(barrier, ring - 1 + plane - 1)

    def send_x(u):
        for d in range(1, NX):
            owner = (x + d) % NX
            remote(
                inp.at[owner // 2, :, :, :, lanes_of(owner, u)],
                xb.at[u, :, :, NX - 1 - d],
                x_send.at[u], x_recv.at[u], at_x(d),
            )

    def send_own(u):
        def body(i):
            d = spread(i, nz)
            remote(
                inp.at[x // 2, :, (z + d) % nz, :, lanes_of(x, u)],
                zb.at[u, :, z, 0],
                z_send.at[u], z_recv.at[u], at_z(d),
            )

        each(nz - 1, body)
        pltpu.make_async_copy(
            inp.at[x // 2, :, z, :, lanes_of(x, u)], zb.at[u, :, z, 0], z_recv.at[u]
        ).start()

    def send_on(u):
        drain(xb.at[u], x_recv.at[u])

        def body(i):
            d = spread(i, nz)
            remote(
                xb.at[u, :, (z + d) % nz],
                zb.at[u, :, z, pl.ds(1, NX - 1)],
                z_send.at[u], z_recv.at[u], at_z(d),
            )

        each(nz - 1, body)
        pltpu.make_async_copy(
            xb.at[u, :, z], zb.at[u, :, z, pl.ds(1, NX - 1)], z_recv.at[u]
        ).start()

    each(PAIRS, send_x)
    each(PAIRS, send_own)
    each(PAIRS, send_on)

    rows = nz * NX * 8
    block = min(rows, 128)
    rate = HD ** (-0.5) * math.log2(math.e)

    def attend(u):
        drain(zb.at[u], z_recv.at[u])
        flat = lambda ref: ref[...].astype(jnp.float32).reshape(-1, LANES)
        keys = flat(zb.at[u, 1]).astype(jnp.bfloat16)
        values = flat(zb.at[u, 2]).astype(jnp.bfloat16)
        per = block // (NX * 8)
        lane = lax.broadcasted_iota(jnp.int32, (block, LANES), 1)

        def body(i, total):
            query = flat(zb.at[u, 0, pl.ds(i * per, per)])
            halves = []
            for head in range(2):
                own = (lane >= HD) == (head == 1)
                scores = lax.dot_general(
                    jnp.where(own, query, 0.0).astype(jnp.bfloat16), keys,
                    (((1,), (1,)), ((), ())), preferred_element_type=jnp.float32,
                )
                raised = jnp.exp2((scores - jnp.max(scores, axis=1, keepdims=True)) * rate)
                share = 1.0 / jnp.sum(raised, axis=1, keepdims=True)
                halves.append(
                    jnp.dot((raised * share).astype(jnp.bfloat16), values, preferred_element_type=jnp.float32)
                )
            result = jnp.where(lane >= HD, halves[1], halves[0])
            rounded = result.reshape(per, NX, 8, LANES).astype(jnp.bfloat16)
            ob[u, pl.ds(i * per, per)] = rounded
            return total + jnp.sum(
                rounded.astype(jnp.float32).reshape(block, LANES), axis=0, keepdims=True
            )

        pool[u] = lax.fori_loop(0, rows // block, body, jnp.zeros((1, LANES), jnp.float32))

    def send_back(u):
        for d in range(1, NX):
            remote(
                ob.at[u, :, d], hb.at[x // 2, :, :, lanes_of(x, u)], h_send.at[u], h_recv.at[u], at_x(d)
            )
        pltpu.make_async_copy(
            ob.at[u, :, 0], hb.at[x // 2, :, :, lanes_of(x, u)], h_recv.at[u]
        ).start()

    def cut(h, last):
        first = PAIRS - 1
        return pl.ds(h * width + (first * LANES if last else 0), LANES if last else first * LANES)

    def send_home(last, begin, end):
        def body(i):
            d = spread(i, nz)
            for h in range(2):
                remote(
                    hb.at[:, (z + d) % nz, :, cut(h, last)],
                    out.at[:, 0, z, :, cut(h, last)],
                    o_send, o_recv, at_z(d),
                )

        span(begin, end, body)

    def keep_home(last):
        for h in range(2):
            pltpu.make_async_copy(hb.at[:, z, :, cut(h, last)], out.at[:, 0, z, :, cut(h, last)], o_recv).start()

    def send_small(src, dst, slot, n, where, k):
        each(n - 1, lambda i: remote(src, dst.at[slot], s_send.at[k], s_recv.at[k], where(far_first(i, n))))
        pltpu.make_async_copy(src, dst.at[slot], s_recv.at[k]).start()

    each(PAIRS - 1, lambda u: (attend(u), send_back(u)))
    attend(PAIRS - 1)

    send_small(pool, zpool, turn, ring, at_ring, 0)
    send_back(PAIRS - 1)
    each(PAIRS - 1, lambda u: drain(ob.at[u], h_recv.at[u]))
    steps = [nz * k // 16 for k in (0, 6, 10)] + [nz - 1]
    send_home(False, steps[0], steps[1])
    keep_home(False)
    drain(zpool, s_recv.at[0])
    for h in range(NH):
        mine[h] = jnp.sum(zpool[pl.ds(h * nz, nz)], axis=0) * (1.0 / (nz * rows))
    send_small(mine, xpool, spot, plane, at_plane, 1)
    send_home(False, steps[1], steps[2])
    drain(xpool, s_recv.at[1])

    partner = pairs[view]
    wanted = (
        (partner // (NH * NC) * NC + partner % NC, partner // NC % NH),
        (y * NC + core, half),
    )
    pooled = [
        jnp.concatenate(
            [xpool[row * NX + 2 * s + h, side, u] for h in range(2) for u in range(PAIRS)], axis=1
        )
        for s, (row, side) in enumerate(wanted)
    ]
    sharp = (exact_dot(unit_vector(pooled[0]), protos[0]) - middle[...]) * (1.0 / tau_teacher)
    soft = exact_dot(unit_vector(pooled[1]), protos[1]) * (1.0 / tau_student)
    top_teacher = jnp.max(sharp, axis=1, keepdims=True)
    raised = jnp.exp(sharp - top_teacher)
    top_student = jnp.max(soft, axis=1, keepdims=True)
    stat[0] = packed(
        (
            top_teacher,
            jnp.sum(raised, axis=1, keepdims=True),
            jnp.sum(raised * soft, axis=1, keepdims=True),
            top_student,
            jnp.sum(jnp.exp(soft - top_student), axis=1, keepdims=True),
        )
    )
    send_small(stat.at[0], zstat, z, nz, at_z, 2)
    send_home(False, steps[2], steps[3])
    drain(ob.at[PAIRS - 1], h_recv.at[PAIRS - 1])
    keep_home(True)
    send_home(True, 0, steps[1])
    drain(zstat, s_recv.at[2])
    stat[1] = packed(merge(zstat[...]))
    send_small(stat.at[1], xstat, x, NX, at_x, 3)
    send_home(True, steps[1], steps[3])
    drain(xstat, s_recv.at[3])
    _, total_teacher, product, best_student, total_student = merge(xstat[...])
    value = best_student + jnp.log(total_student) - product / total_teacher
    loss[0] = jnp.sum(value)

    def finish(u):
        drain(xb.at[u], x_send.at[u])
        drain(zb.at[u, :, pl.ds(0, nz - 1)], z_send.at[u])
        drain(ob.at[u, :, pl.ds(0, NX - 1)], h_send.at[u])

    each(PAIRS, finish)
    drain(zpool.at[pl.ds(0, ring - 1)], s_send.at[0])
    drain(xpool.at[pl.ds(0, plane - 1)], s_send.at[1])
    drain(zstat.at[pl.ds(0, nz - 1)], s_send.at[2])
    drain(xstat.at[pl.ds(0, NX - 1)], s_send.at[3])
    drain(hb.at[:, pl.ds(0, nz - 1)], o_send)
    drain(out, o_recv)


def local(nz, ndp, qkv_teacher, qkv_student, proto_teacher, proto_student, center, pairing):
    frames, rows, features = qkv_teacher.shape[2:]
    bf16, f32 = jnp.bfloat16, jnp.float32
    dma = pltpu.SemaphoreType.DMA
    anywhere = pl.BlockSpec(memory_space=pl.ANY)
    smem = pl.BlockSpec(memory_space=pltpu.SMEM)
    out, loss = pl.pallas_call(
        functools.partial(kernel, nz, ndp),
        out_shape=(
            jax.ShapeDtypeStruct((2, 1, frames, rows, features), bf16),
            jax.ShapeDtypeStruct((1,), f32),
        ),
        in_specs=[anywhere] * 6,
        out_specs=(anywhere, smem),
        scratch_shapes=[
            pltpu.VMEM((2, 3, frames, rows, features), bf16),
            pltpu.VMEM((2, features, LANES), bf16),
            pltpu.VMEM((1, LANES), f32),
            pltpu.SMEM((ndp,), jnp.int32),
            pltpu.VMEM((PAIRS, 3, nz, NX - 1, rows, LANES), bf16),
            pltpu.VMEM((PAIRS, 3, nz, NX, rows, LANES), bf16),
            pltpu.VMEM((PAIRS, nz, NX, rows, LANES), bf16),
            pltpu.VMEM((2, nz, rows, features), bf16),
            pltpu.VMEM((PAIRS, 1, LANES), f32),
            pltpu.VMEM((NH * nz, PAIRS, 1, LANES), f32),
            pltpu.VMEM((NH, PAIRS, 1, LANES), f32),
            pltpu.VMEM((ndp // NH * NX, NH, PAIRS, 1, LANES), f32),
            pltpu.VMEM((2, 1, LANES), f32),
            pltpu.VMEM((nz, 1, LANES), f32),
            pltpu.VMEM((NX, 1, LANES), f32),
            dma((6,)),
            dma((PAIRS,)), dma((PAIRS,)),
            dma((PAIRS,)), dma((PAIRS,)),
            dma((PAIRS,)), dma((PAIRS,)),
            dma(()), dma(()),
            dma((4,)), dma((4,)),
        ],
        compiler_params=pltpu.CompilerParams(
            collective_id=0, has_side_effects=True, vmem_limit_bytes=58 * 1024 * 1024
        ),
        name="views",
    )(qkv_teacher, qkv_student, proto_teacher, proto_student, center.reshape(1, -1), pairing)
    return out[0], out[1], loss


def solution(mesh):
    wide = P("dp", None, None, "seq", None)
    return jax.shard_map(
        functools.partial(local, mesh.shape["seq"] // NX, mesh.shape["dp"]),
        mesh=mesh,
        in_specs=(wide, wide, P(None, "seq"), P(None, "seq"), P("seq"), P()),
        out_specs=(P("dp", None, "seq", None), P("dp", None, "seq", None), P("dp")),
        check_vma=False,
    )
```

```python
import functools
import math

import jax
import jax.numpy as jnp
from jax import lax
from jax.experimental import pallas as pl
from jax.experimental.pallas import tpu as pltpu
from jax.sharding import PartitionSpec as P

HD = 64
NX = 4
NH, NC = 2, 2
PAIRS = 3
LANES = 128

tau_teacher = 0.07
tau_student = 0.1
norm_eps = 1e-06


def spread(step, n):
    return 1 + (n // 2 - 1 + step * (n // 4 if n >= 16 else 1)) % (n - 1)


def drain(ref, sem):
    pltpu.make_async_copy(ref, ref, sem).wait()


def unit_vector(values):
    return values * lax.rsqrt(jnp.mean(values * values) + norm_eps)


def exact_dot(row, matrix):
    high = row.astype(jnp.bfloat16).astype(jnp.float32)
    rest = row - high
    middle = rest.astype(jnp.bfloat16).astype(jnp.float32)
    low = rest - middle
    index = lax.broadcasted_iota(jnp.int32, (8, row.shape[1]), 0)
    parts = jnp.where(index == 0, high, jnp.where(index == 1, middle, jnp.where(index == 2, low, 0.0)))
    products = jnp.dot(parts.astype(jnp.bfloat16), matrix, preferred_element_type=jnp.float32)
    return jnp.sum(products, axis=0, keepdims=True)


def merge(stats):
    lane = lax.broadcasted_iota(jnp.int32, stats.shape, 2)

    def column(i):
        return jnp.sum(jnp.where(lane == i, stats, 0.0), axis=2, keepdims=True)

    top_teacher, top_student = column(0), column(3)
    best_teacher = jnp.max(top_teacher, axis=0, keepdims=True)
    best_student = jnp.max(top_student, axis=0, keepdims=True)
    weight = jnp.exp(top_teacher - best_teacher)
    share = jnp.exp(top_student - best_student)
    return (
        best_teacher[0],
        jnp.sum(column(1) * weight, axis=0),
        jnp.sum(column(2) * weight, axis=0),
        best_student[0],
        jnp.sum(column(4) * share, axis=0),
    )


def packed(values):
    lane = lax.broadcasted_iota(jnp.int32, (1, LANES), 1)
    row = jnp.zeros((1, LANES), jnp.float32)
    for i, value in enumerate(values):
        row = jnp.where(lane == i, value, row)
    return row


def kernel(
    nz, ndp,
    qkv_t, qkv_s, proto_t, proto_s, center, pairing,
    out, loss,
    inp, protos, middle, pairs, xb, zb, ob, hb, pool, zpool, mine, xpool, stat, zstat,
    in_sem, x_send, x_recv, z_send, z_recv, h_send, h_recv, o_send, o_recv, s_send, s_recv, p_send, p_recv,
):
    view = lax.axis_index("dp")
    me = lax.axis_index("seq")
    x = me % NX
    z = me // NX
    y, half, core = view // (NH * NC), view // NC % NH, view % NC
    ring, turn = NH * nz, half * nz + z
    plane, spot = ndp // NH * NX, (y * NC + core) * NX + x
    width = PAIRS * LANES

    def at_x(d):
        return {"seq": z * NX + (x + d) % NX}

    def at_z(d):
        return {"seq": (z + d) % nz * NX + x}

    def at_ring(d):
        to = (turn + d) % ring
        return {"dp": (y * NH + to // nz) * NC + core, "seq": to % nz * NX + x}

    def at_plane(d):
        to = (spot + d) % plane
        row = to // NX
        return {"dp": (row // NC * NH + half) * NC + row % NC, "seq": z * NX + to % NX}

    def lanes_of(owner, u):
        return pl.ds(pl.multiple_of(owner % 2 * width + u * LANES, LANES), LANES)

    def remote(src, dst, send, recv, where):
        pltpu.make_async_remote_copy(
            src_ref=src, dst_ref=dst, send_sem=send, recv_sem=recv,
            device_id=where, device_id_type=pl.DeviceIdType.MESH,
        ).start()

    def span(first, last, body):
        lax.fori_loop(first, last, lambda i, c: (body(i), c)[1], 0)

    def each(n, body):
        span(0, n, body)

    def far_first(i, n):
        return 1 + (n // 2 - 1 + i) % (n - 1)

    barrier = pltpu.get_barrier_semaphore()

    def greet(where):
        pl.semaphore_signal(barrier, inc=1, device_id=where, device_id_type=pl.DeviceIdType.MESH)

    each(ring - 1, lambda i: greet(at_ring(far_first(i, ring))))
    each(plane - 1, lambda i: greet(at_plane(i + 1)))
    loads = [
        pltpu.make_async_copy(src, dst, in_sem.at[i])
        for i, (src, dst) in enumerate(
            (
                (qkv_t, inp.at[pl.ds(0, 1)]),
                (qkv_s, inp.at[pl.ds(1, 1)]),
                (proto_t, protos.at[0, x]),
                (proto_s, protos.at[1, x]),
                (center, middle.at[x]),
                (pairing, pairs),
            )
        )
    ]
    for load in loads:
        load.start()
    for load in loads:
        load.wait()
    pl.semaphore_wait(barrier, ring - 1 + plane - 1)

    def send_x(u):
        for d in range(1, NX):
            owner = (x + d) % NX
            remote(
                inp.at[owner // 2, :, :, :, lanes_of(owner, u)],
                xb.at[u, :, :, NX - 1 - d],
                x_send.at[u], x_recv.at[u], at_x(d),
            )

    def send_own(u):
        def body(i):
            d = spread(i, nz)
            remote(
                inp.at[x // 2, :, (z + d) % nz, :, lanes_of(x, u)],
                zb.at[u, :, z, 0],
                z_send.at[u], z_recv.at[u], at_z(d),
            )

        each(nz - 1, body)
        pltpu.make_async_copy(
            inp.at[x // 2, :, z, :, lanes_of(x, u)], zb.at[u, :, z, 0], z_recv.at[u]
        ).start()

    def send_on(u):
        drain(xb.at[u], x_recv.at[u])

        def body(i):
            d = spread(i, nz)
            remote(
                xb.at[u, :, (z + d) % nz],
                zb.at[u, :, z, pl.ds(1, NX - 1)],
                z_send.at[u], z_recv.at[u], at_z(d),
            )

        each(nz - 1, body)
        pltpu.make_async_copy(
            xb.at[u, :, z], zb.at[u, :, z, pl.ds(1, NX - 1)], z_recv.at[u]
        ).start()

    each(PAIRS, send_x)
    each(PAIRS, send_own)
    for d in range(1, NX):
        remote(protos.at[:, x], protos.at[:, x], p_send.at[0], p_recv.at[0], at_x(d))
        remote(middle.at[x], middle.at[x], p_send.at[1], p_recv.at[1], at_x(d))
    each(PAIRS, send_on)

    rows = nz * NX * 8
    block = min(rows, 128)
    rate = HD ** (-0.5) * math.log2(math.e)

    def attend(u):
        drain(zb.at[u], z_recv.at[u])
        flat = lambda ref: ref[...].astype(jnp.float32).reshape(-1, LANES)
        keys = flat(zb.at[u, 1]).astype(jnp.bfloat16)
        values = flat(zb.at[u, 2]).astype(jnp.bfloat16)
        per = block // (NX * 8)
        lane = lax.broadcasted_iota(jnp.int32, (block, LANES), 1)

        def body(i, total):
            query = flat(zb.at[u, 0, pl.ds(i * per, per)])
            halves = []
            for head in range(2):
                own = (lane >= HD) == (head == 1)
                scores = lax.dot_general(
                    jnp.where(own, query, 0.0).astype(jnp.bfloat16), keys,
                    (((1,), (1,)), ((), ())), preferred_element_type=jnp.float32,
                )
                raised = jnp.exp2((scores - jnp.max(scores, axis=1, keepdims=True)) * rate)
                share = 1.0 / jnp.sum(raised, axis=1, keepdims=True)
                halves.append(
                    jnp.dot((raised * share).astype(jnp.bfloat16), values, preferred_element_type=jnp.float32)
                )
            result = jnp.where(lane >= HD, halves[1], halves[0])
            rounded = result.reshape(per, NX, 8, LANES).astype(jnp.bfloat16)
            ob[u, pl.ds(i * per, per)] = rounded
            return total + jnp.sum(
                rounded.astype(jnp.float32).reshape(block, LANES), axis=0, keepdims=True
            )

        pool[u] = lax.fori_loop(0, rows // block, body, jnp.zeros((1, LANES), jnp.float32))

    def send_back(u):
        for d in range(1, NX):
            remote(
                ob.at[u, :, d], hb.at[x // 2, :, :, lanes_of(x, u)], h_send.at[u], h_recv.at[u], at_x(d)
            )
        pltpu.make_async_copy(
            ob.at[u, :, 0], hb.at[x // 2, :, :, lanes_of(x, u)], h_recv.at[u]
        ).start()

    def cut(h, last):
        first = PAIRS - 1
        return pl.ds(h * width + (first * LANES if last else 0), LANES if last else first * LANES)

    def send_home(last, begin, end):
        def body(i):
            d = spread(i, nz)
            for h in range(2):
                remote(
                    hb.at[:, (z + d) % nz, :, cut(h, last)],
                    out.at[:, 0, z, :, cut(h, last)],
                    o_send, o_recv, at_z(d),
                )

        span(begin, end, body)

    def keep_home(last):
        for h in range(2):
            pltpu.make_async_copy(hb.at[:, z, :, cut(h, last)], out.at[:, 0, z, :, cut(h, last)], o_recv).start()

    def send_small(src, dst, slot, n, where, k):
        each(n - 1, lambda i: remote(src, dst.at[slot], s_send.at[k], s_recv.at[k], where(far_first(i, n))))
        pltpu.make_async_copy(src, dst.at[slot], s_recv.at[k]).start()

    each(PAIRS - 1, lambda u: (attend(u), send_back(u)))
    attend(PAIRS - 1)

    send_small(pool, zpool, turn, ring, at_ring, 0)
    send_back(PAIRS - 1)
    each(PAIRS - 1, lambda u: drain(ob.at[u], h_recv.at[u]))
    send_home(False, 0, nz - 1)
    keep_home(False)
    drain(zpool, s_recv.at[0])
    for h in range(NH):
        mine[h] = jnp.sum(zpool[pl.ds(h * nz, nz)], axis=0) * (1.0 / (nz * rows))
    send_small(mine, xpool, spot, plane, at_plane, 1)
    drain(ob.at[PAIRS - 1], h_recv.at[PAIRS - 1])
    keep_home(True)
    send_home(True, 0, nz - 1)
    drain(xpool, s_recv.at[1])

    partner = pairs[view]
    wanted = (
        (partner // (NH * NC) * NC + partner % NC, partner // NC % NH),
        (y * NC + core, half),
    )
    pooled = [
        jnp.concatenate(
            [xpool[row * NX + 2 * s + h, side, u] for h in range(2) for u in range(PAIRS)], axis=1
        )
        for s, (row, side) in enumerate(wanted)
    ]
    drain(protos.at[:, pl.ds(0, NX - 1)], p_recv.at[0])
    drain(middle.at[pl.ds(0, NX - 1)], p_recv.at[1])
    units = [unit_vector(row) for row in pooled]

    def over_x(parts):
        return jnp.concatenate([parts(i) for i in range(NX)], axis=1)

    sharp = (over_x(lambda i: exact_dot(units[0], protos[0, i])) - over_x(lambda i: middle[i])) * (
        1.0 / tau_teacher
    )
    soft = over_x(lambda i: exact_dot(units[1], protos[1, i])) * (1.0 / tau_student)
    top_teacher = jnp.max(sharp, axis=1, keepdims=True)
    raised = jnp.exp(sharp - top_teacher)
    top_student = jnp.max(soft, axis=1, keepdims=True)
    stat[...] = packed(
        (
            top_teacher,
            jnp.sum(raised, axis=1, keepdims=True),
            jnp.sum(raised * soft, axis=1, keepdims=True),
            top_student,
            jnp.sum(jnp.exp(soft - top_student), axis=1, keepdims=True),
        )
    )
    send_small(stat, zstat, z, nz, at_z, 2)
    drain(zstat, s_recv.at[2])
    _, total_teacher, product, best_student, total_student = merge(zstat[...])
    value = best_student + jnp.log(total_student) - product / total_teacher
    loss[0] = jnp.sum(value)

    def finish(u):
        drain(xb.at[u], x_send.at[u])
        drain(zb.at[u, :, pl.ds(0, nz - 1)], z_send.at[u])
        drain(ob.at[u, :, pl.ds(0, NX - 1)], h_send.at[u])

    each(PAIRS, finish)
    drain(zpool.at[pl.ds(0, ring - 1)], s_send.at[0])
    drain(xpool.at[pl.ds(0, plane - 1)], s_send.at[1])
    drain(zstat.at[pl.ds(0, nz - 1)], s_send.at[2])
    drain(protos.at[:, pl.ds(0, NX - 1)], p_send.at[0])
    drain(middle.at[pl.ds(0, NX - 1)], p_send.at[1])
    drain(hb.at[:, pl.ds(0, nz - 1)], o_send)
    drain(out, o_recv)


def local(nz, ndp, qkv_teacher, qkv_student, proto_teacher, proto_student, center, pairing):
    frames, rows, features = qkv_teacher.shape[2:]
    bf16, f32 = jnp.bfloat16, jnp.float32
    dma = pltpu.SemaphoreType.DMA
    anywhere = pl.BlockSpec(memory_space=pl.ANY)
    smem = pl.BlockSpec(memory_space=pltpu.SMEM)
    out, loss = pl.pallas_call(
        functools.partial(kernel, nz, ndp),
        out_shape=(
            jax.ShapeDtypeStruct((2, 1, frames, rows, features), bf16),
            jax.ShapeDtypeStruct((1,), f32),
        ),
        in_specs=[anywhere] * 6,
        out_specs=(anywhere, smem),
        scratch_shapes=[
            pltpu.VMEM((2, 3, frames, rows, features), bf16),
            pltpu.VMEM((2, NX, features, LANES), bf16),
            pltpu.VMEM((NX, 1, LANES), f32),
            pltpu.SMEM((ndp,), jnp.int32),
            pltpu.VMEM((PAIRS, 3, nz, NX - 1, rows, LANES), bf16),
            pltpu.VMEM((PAIRS, 3, nz, NX, rows, LANES), bf16),
            pltpu.VMEM((PAIRS, nz, NX, rows, LANES), bf16),
            pltpu.VMEM((2, nz, rows, features), bf16),
            pltpu.VMEM((PAIRS, 1, LANES), f32),
            pltpu.VMEM((NH * nz, PAIRS, 1, LANES), f32),
            pltpu.VMEM((NH, PAIRS, 1, LANES), f32),
            pltpu.VMEM((ndp // NH * NX, NH, PAIRS, 1, LANES), f32),
            pltpu.VMEM((1, LANES), f32),
            pltpu.VMEM((nz, 1, LANES), f32),
            dma((6,)),
            dma((PAIRS,)), dma((PAIRS,)),
            dma((PAIRS,)), dma((PAIRS,)),
            dma((PAIRS,)), dma((PAIRS,)),
            dma(()), dma(()),
            dma((3,)), dma((3,)),
            dma((2,)), dma((2,)),
        ],
        compiler_params=pltpu.CompilerParams(
            collective_id=0, has_side_effects=True, vmem_limit_bytes=58 * 1024 * 1024
        ),
        name="views",
    )(qkv_teacher, qkv_student, proto_teacher, proto_student, center.reshape(1, -1), pairing)
    return out[0], out[1], loss


def solution(mesh):
    wide = P("dp", None, None, "seq", None)
    return jax.shard_map(
        functools.partial(local, mesh.shape["seq"] // NX, mesh.shape["dp"]),
        mesh=mesh,
        in_specs=(wide, wide, P(None, "seq"), P(None, "seq"), P("seq"), P()),
        out_specs=(P("dp", None, "seq", None), P("dp", None, "seq", None), P("dp")),
        check_vma=False,
    )
```
